256 devices in a mesh: section: 32 (over y, x, z_lo), tensor: 8 (over z_hi, core).
Axes of the slice: x: 4, y: 4, z: 8 (z_hi: 4, z_lo: 2; z = z_hi * 2 + z_lo), core: 2. Of those that a mesh axis runs over, the one named last changes fastest.
Arguments:
- stashed_qk: bfloat16 [32, 2, 512, 6144], P('section', None, None, 'tensor'), may hold values from -24 to 24
- grad_heads: bfloat16 [32, 512, 6144], P('section', None, 'tensor'), may hold values from -6 to 6
- segment_ids: int32 [32, 512], replicated, may hold values from 0 to 3, never falling along the last dimension, each value on 1 to 256 neighbouring positions
- w_value: bfloat16 [32, 6144, 6144], P('section', None, 'tensor'), may hold values from -0.078125 to 0.078125
- grad_in: bfloat16 [32, 512, 6144], P('section', 'tensor'), may hold values from -4 to 4
Outputs:
- upstream: bfloat16 [32, 512, 6144], P('section', 'tensor')
The draws below stay inside these ranges and needn't reach their ends.
All inputs are finite; a program needn't handle non-finite values.
Results may differ from the reference program's by a relative error of at most 0.02.
Values may be sent and summed in bfloat16 or wider, within the bound.
No kernel may reach another device: no remote copies, remote signals or barrier semaphores. Data moves between devices by JAX's collectives and lax.ppermute only.
A program may use at most 64 MiB of HBM per device.

```python
import math
import jax
import jax.numpy as jnp
import numpy as np
from jax import lax

FEAT = 6144
HEADS = 48
HD = 128
TOK = 512
SEGMENTS = 4
SECTIONS = 32
N_TENSOR = 8


def draw_stashed_qk(key, part):
    key = jax.random.fold_in(key, 7)
    first_key = jax.random.fold_in(key, 0)
    full_shape = (SECTIONS, 2, TOK, HEADS * HD)
    base_draw = jnp.clip(jax.random.normal(first_key, full_shape, jnp.float32), -6.0, 6.0)
    return base_draw.astype(jnp.bfloat16)


def levels(rng, shape, pieces, smallest, top_value):
    loudness = 1.0
    for position, parts in pieces:
        draws = jax.random.uniform(jax.random.fold_in(jax.random.fold_in(rng, 6), position), (parts,), jnp.float32, smallest / len(pieces), top_value / len(pieces))
        loudness = loudness * jnp.repeat(jnp.exp(draws), shape[position] // parts).reshape((-1,) + (1,) * (len(shape) - 1 - position))
    return loudness


def length_profile(amount, total, reach, slope):
    loads = [(1 << 20) // math.isqrt(standing ** slope) + 1 for standing in range(2, amount + 1)]
    rest, holding = total - reach - (amount - 1), [1] * (amount - 1)
    while rest > 0:
        candidates = [i for i in range(amount - 1) if holding[i] < reach]
        pool, remaining = sum([loads[i] for i in candidates]), rest
        for i in candidates:
            more = min(reach - holding[i], max(1, remaining * loads[i] // pool), rest)
            holding[i] = holding[i] + more
            rest = rest - more
    return np.array([reach] + holding)


def ragged_sizes(rng, number_of, total, reach, lean):
    if number_of == 2:
        one = jax.random.randint(rng, (), max(1, total - reach), min(reach, total - 1) + 1)
        return jnp.stack([one, total - one])
    lengths = jnp.asarray(length_profile(number_of, total, reach, lean), jnp.int32)
    twos = (number_of - 1) // 2
    donor, taker = lengths[1:1 + 2 * twos:2], lengths[2:2 + 2 * twos:2]
    slack = jnp.minimum(donor - 1, reach - taker)
    shifted = jax.random.randint(jax.random.fold_in(rng, 1), (twos,), 0, 1 << 20) % (slack + 1)
    lengths = lengths.at[1:1 + 2 * twos:2].set(donor - shifted).at[2:2 + 2 * twos:2].set(taker + shifted)
    return lengths[jax.random.permutation(jax.random.fold_in(rng, 2), number_of)]


def noise(own_key, extent, scale, limit, shards=(), kind=jnp.bfloat16):
    result = scale * jax.random.normal(own_key, extent, jnp.float32)
    if shards:
        result = result * levels(own_key, extent, shards, -0.22, 0.18)
    return jnp.clip(result, -limit, limit).astype(kind)


def setup_inputs(seed: int = 0) -> dict:
    key_list = jax.random.split(jax.random.key(seed), 6)
    stashed_qk = draw_stashed_qk(jax.random.fold_in(key_list[5], 71), 0)
    grad_heads = noise(key_list[1], (SECTIONS, TOK, HEADS * HD), 1.0, 6.0, ((0, 32), (2, 8)))
    segment_ids = jax.vmap(lambda own: jnp.searchsorted(jnp.cumsum(ragged_sizes(own, SEGMENTS, TOK, TOK // 2, 0)), jnp.arange(TOK), side="right"))(jax.random.split(key_list[2], SECTIONS)).reshape((SECTIONS, TOK)).astype(jnp.int32)
    w_value = noise(key_list[3], (SECTIONS, FEAT, HEADS * HD), (HEADS * HD) ** -0.5, 0.078125, ((0, 32), (2, 8)))
    grad_in = noise(key_list[4], (SECTIONS, TOK, FEAT), 0.25, 4.0, ((0, 32), (1, 8)))
    return dict(stashed_qk=stashed_qk, grad_heads=grad_heads, segment_ids=segment_ids, w_value=w_value, grad_in=grad_in)


def value_gradient(queries, key_rows, grad_heads, segment_row):
    row_count = queries.shape[0]
    head_count = queries.shape[1] // HD
    query_heads = queries.reshape(row_count, head_count, HD).astype(jnp.float32)
    key_heads = key_rows.reshape(row_count, head_count, HD).astype(jnp.float32)
    grad_split = grad_heads.reshape(row_count, head_count, HD).astype(jnp.float32)
    scores = jnp.einsum("qhd,khd->hqk", query_heads, key_heads) * (HD ** -0.5)
    positions = jnp.arange(row_count, dtype=jnp.int32)
    visible = (positions[None, :] <= positions[:, None]) & (segment_row[None, :] == segment_row[:, None])
    scores = jnp.where(visible[None], scores, -1e30)
    largest = jnp.max(scores, axis=2, keepdims=True)
    raised = jnp.exp(scores - largest)
    softmax_out = (raised / jnp.sum(raised, axis=2, keepdims=True)).astype(jnp.bfloat16)
    value_grad = jnp.einsum("hqk,qhd->khd", softmax_out.astype(jnp.float32), grad_split)
    return value_grad.astype(jnp.bfloat16).reshape(row_count, head_count * HD)


def section_gradient(operands):
    stashed, grad_heads, segment_row, weight, residual = operands
    value_grad = value_gradient(stashed[0], stashed[1], grad_heads, segment_row)
    group_width = value_grad.shape[1] // N_TENSOR
    grouped = value_grad.reshape(TOK, N_TENSOR, group_width).astype(jnp.float32)
    weight_grouped = weight.reshape(FEAT, N_TENSOR, group_width).astype(jnp.float32)
    partials = jnp.einsum("tng,fng->ntf", grouped, weight_grouped).astype(jnp.bfloat16)
    partials = lax.optimization_barrier(partials)
    attention = jnp.sum(partials.astype(jnp.float32), axis=0).astype(jnp.bfloat16)
    attention = lax.optimization_barrier(attention)
    return (attention.astype(jnp.float32) + residual.astype(jnp.float32)).astype(jnp.bfloat16)


def reference(stashed_qk, grad_heads, segment_ids, w_value, grad_in):
    layer_grad = lax.map(section_gradient, (stashed_qk[::-1], grad_heads, segment_ids, w_value, grad_in))
    tail_zeros = jnp.zeros((1, TOK, FEAT), jnp.bfloat16)
    return jnp.concatenate([layer_grad[1:], tail_zeros], axis=0)
```

```python
import jax
import jax.numpy as jnp
from jax import lax
from jax.sharding import PartitionSpec as P

HD = 128
TOK = 512
FEAT = 6144
AXES = ("section", "tensor")
PIECES = 4


def place_of(device):
    section, tensor = divmod(device, 8)
    return section // 8, section // 2 % 4, tensor // 2 * 2 + section % 2, tensor % 2


def device_at(y, x, z, core):
    section = (y % 4) * 8 + (x % 4) * 2 + z % 2
    return section * 8 + z % 8 // 2 * 2 + core


def sent(value, target):
    pairs = []
    for device in range(256):
        place = target(*place_of(device))
        if place is not None:
            pairs.append((device, device_at(*place)))
    return lax.ppermute(value, AXES, pairs)


def mirror(y, x, z, core):
    return 3 - y, 3 - x, z ^ 1, core


def other_core(y, x, z, core):
    return y, x, z, 1 - core


def along_z(by):
    return lambda y, x, z, core: (y, x, z + by, core)


def previous(y, x, z, flip):
    if z % 2 == 0:
        return (y, x, z) if flip else None
    if x > 0:
        return y, x - 1, z
    return (y - 1, 3, z) if y > 0 else None


def to_previous(flip):
    def target(y, x, z, core):
        place = previous(y, x, z, flip)
        return None if place is None else place + (core ^ flip,)

    return target


def value_gradient(queries, key_rows, grad_heads, segment_row):
    row_count = queries.shape[0]
    head_count = queries.shape[1] // HD
    query_heads = queries.reshape(row_count, head_count, HD)
    key_heads = key_rows.reshape(row_count, head_count, HD)
    grad_split = grad_heads.reshape(row_count, head_count, HD)
    scores = jnp.einsum(
        "qhd,khd->hqk", query_heads, key_heads, preferred_element_type=jnp.float32
    ) * HD ** (-0.5)
    positions = jnp.arange(row_count, dtype=jnp.int32)
    visible = (positions[None, :] <= positions[:, None]) & (
        segment_row[None, :] == segment_row[:, None]
    )
    scores = jnp.where(visible[None], scores, -1e30)
    largest = jnp.max(scores, axis=2, keepdims=True)
    raised = jnp.exp(scores - largest)
    softmax_out = (raised / jnp.sum(raised, axis=2, keepdims=True)).astype(jnp.bfloat16)
    value_grad = jnp.einsum(
        "hqk,qhd->khd", softmax_out, grad_split, preferred_element_type=jnp.float32
    )
    return value_grad.astype(jnp.bfloat16).reshape(row_count, head_count * HD)


def body(stashed_qk, grad_heads, segment_ids, w_value, grad_in):
    section = lax.axis_index("section")
    tensor = lax.axis_index("tensor")
    z_low, z_high, core = section % 2, tensor // 2, tensor % 2
    half = FEAT // 2
    piece = half // PIECES

    stashed = sent(stashed_qk[0], mirror)

    weight = w_value[0]
    kept = lax.dynamic_slice_in_dim(weight, core * half, half, 0)
    given = lax.dynamic_slice_in_dim(weight, (1 - core) * half, half, 0)
    taken = sent(given, other_core)
    rows = grad_in[0]
    residual_kept = lax.dynamic_slice_in_dim(rows, core * half, half, 1)
    residual_taken = sent(lax.dynamic_slice_in_dim(rows, (1 - core) * half, half, 1), other_core)
    residual = jnp.where(
        core == 0,
        jnp.concatenate([residual_kept, residual_taken], 0),
        jnp.concatenate([residual_taken, residual_kept], 0),
    )

    segment_row = lax.dynamic_index_in_dim(segment_ids, section, 0, keepdims=False)
    own_grad = value_gradient(stashed[0], stashed[1], grad_heads[0], segment_row)
    other_grad = sent(own_grad, other_core)
    value_grad = jnp.concatenate([own_grad, other_grad], 1)
    base = (z_high + z_low) * 128 % TOK
    value_grad = lax.dynamic_slice_in_dim(
        jnp.concatenate([value_grad, value_grad], 0), base, TOK, 0
    )
    joined = jnp.concatenate([kept, taken], 1)

    def product(rows, columns):
        return lax.dot_general(
            rows, columns, (((1,), (1,)), ((), ())), preferred_element_type=jnp.float32
        )

    far = []
    for n in range(PIECES):
        columns = joined[n * piece : (n + 1) * piece]
        sums = product(value_grad[128:384], columns).astype(jnp.bfloat16)
        far.append((sent(sums[:128], along_z(2)), sent(sums[128:], along_z(-2))))
    near = []
    for n in range(PIECES):
        columns = joined[n * piece : (n + 1) * piece]
        added = residual[:, n * piece : (n + 1) * piece].astype(jnp.float32)
        up = product(value_grad[:128], columns) + far[n][0].astype(jnp.float32)
        down = product(value_grad[384:], columns) + far[n][1].astype(jnp.float32)
        up = up + jnp.where(z_low == 0, added, 0.0)
        down = down + jnp.where(z_low == 1, added, 0.0)
        near.append(
            (
                sent(up.astype(jnp.bfloat16), along_z(1)),
                sent(down.astype(jnp.bfloat16), along_z(-1)),
            )
        )
    straight, crossed = [], []
    for n in range(PIECES):
        total = (near[n][0].astype(jnp.float32) + near[n][1].astype(jnp.float32)).astype(jnp.bfloat16)
        same = lax.dynamic_slice_in_dim(total, core * 64, 64, 0)
        cross = lax.dynamic_slice_in_dim(total, (1 - core) * 64, 64, 0)
        straight.append(jnp.where(z_low == 0, same, sent(same, to_previous(0))))
        crossed.append(sent(cross, to_previous(1)))
    straight = jnp.concatenate(straight, 1)
    crossed = jnp.concatenate(crossed, 1)
    return jnp.where(
        core == 0,
        jnp.concatenate([straight, crossed], 1),
        jnp.concatenate([crossed, straight], 1),
    )[None]


def solution(mesh):
    in_specs = (
        P("section", None, None, "tensor"),
        P("section", None, "tensor"),
        P(),
        P("section", None, "tensor"),
        P("section", "tensor", None),
    )
    out_specs = P("section", "tensor", None)
    return jax.shard_map(body, mesh=mesh, in_specs=in_specs, out_specs=out_specs, check_vma=False)
```

```python
import functools

import jax
import jax.numpy as jnp
from jax import lax
from jax.experimental import pallas as pl
from jax.experimental.pallas import tpu as pltpu
from jax.sharding import PartitionSpec as P

HD = 128
TOK = 512
FEAT = 6144
AXES = ("section", "tensor")
GROUPS = ((0, 3), (3, 3))
PIECES = 4
TILE = 768
BLOCK = 128
BLOCKS = TOK // BLOCK
NT = (((1,), (1,)), ((), ()))
NN = (((1,), (0,)), ((), ()))
VMEM = 48 * 1024 * 1024


def place_of(device):
    section, tensor = divmod(device, 8)
    return section // 8, section // 2 % 4, tensor // 2 * 2 + section % 2, tensor % 2


def device_at(y, x, z, core):
    section = (y % 4) * 8 + (x % 4) * 2 + z % 2
    return section * 8 + z % 8 // 2 * 2 + core


def sent(value, target):
    pairs = []
    for device in range(256):
        place = target(*place_of(device))
        if place is not None:
            pairs.append((device, device_at(*place)))
    return lax.ppermute(value, AXES, pairs)


def mirror(y, x, z, core):
    return 3 - y, 3 - x, z ^ 1, core


def other_core(y, x, z, core):
    return y, x, z, 1 - core


def along_z(by):
    return lambda y, x, z, core: (y, x, z + by, core)


def to_previous(by):
    def target(y, x, z, core):
        if z % 2 == 1:
            return y, x, z + by, core
        if x > 0:
            return y, x - 1, z + by, core
        return (y - 1, 3, z + by, core) if y > 0 else None

    return target


def iota(shape, dim, start=0):
    return lax.broadcasted_iota(jnp.int32, shape, dim) + start


def boundaries(row):
    return [
        jnp.sum(jnp.where(row < n, 1.0, 0.0), axis=1, keepdims=True).astype(jnp.int32)
        for n in (1, 2, 3)
    ]


def starts(bounds, positions):
    found = jnp.zeros_like(positions)
    for bound in bounds:
        found = jnp.where(positions >= bound, bound, found)
    return found


def dot(left, right, dims=NN):
    return lax.dot_general(left, right, dims, preferred_element_type=jnp.float32)


def one_hot(condition):
    return jnp.where(condition, 1.0, 0.0).astype(jnp.bfloat16)


def window(n):
    low = max(n - 2, 0)
    return low, n - low + 1


def seen(bounds, n):
    low, count = window(n)
    keys = iota((count * BLOCK, BLOCK), 0, low * BLOCK)
    rows = iota((1, BLOCK), 1, n * BLOCK)
    return (keys >= starts(bounds, rows)) & (keys <= rows)


def pack_kernel(heads, place_ref, stash_ref, segment_ref, out_ref, over_ref, diagonal_ref):
    bounds = boundaries(segment_ref[pl.ds(place_ref[0], 1), :])
    below = iota((BLOCK, BLOCK), 0) < iota((BLOCK, BLOCK), 1)
    level = iota((BLOCK, BLOCK), 0) == iota((BLOCK, BLOCK), 1)
    above = iota((BLOCK, BLOCK), 0) > iota((BLOCK, BLOCK), 1)
    diagonal_ref[...] = jnp.zeros_like(diagonal_ref)
    factor = HD ** (-0.5) * 1.4426950408889634
    for n in range(BLOCKS):
        low, count = window(n)
        here = slice(n * BLOCK, (n + 1) * BLOCK)
        bias = jnp.where(seen(bounds, n), 0.0, -1e30)
        if n:
            columns = iota((1, n * BLOCK - low * BLOCK), 1, low * BLOCK)
            shifted = iota((BLOCK, 1), 0) + columns - 2 * starts(bounds, columns) - 127
            folding = one_hot((shifted & 127) == 0)
        for h in range(heads):
            features = slice(h * HD, (h + 1) * HD)
            keys = stash_ref[0, 1, low * BLOCK : (n + 1) * BLOCK, features]
            scores = dot(keys, stash_ref[0, 0, here, features], NT) + bias
            largest = jnp.max(scores, axis=0, keepdims=True)
            raised = jnp.exp2((scores - largest) * factor)
            probs = raised * (1.0 / jnp.sum(raised, axis=0, keepdims=True))
            last = probs[(count - 1) * BLOCK :]
            second = probs[(count - 2) * BLOCK : (count - 1) * BLOCK] if n else None
            first = probs[:BLOCK] if n > 1 else None
            diagonal_ref[h : h + 1, here] = jnp.sum(
                jnp.where(level, last, 0.0), axis=0, keepdims=True
            )
            kept = jnp.where(below, last, second if n else 0.0)
            out_ref[features, here] = kept.astype(jnp.bfloat16)
            if n:
                over = jnp.where(below, second, 0.0).astype(jnp.bfloat16)
                if n > 1:
                    over = jnp.concatenate(
                        [jnp.where(above, first, 0.0).astype(jnp.bfloat16), over], 0
                    )
                over_ref[features, (n - 1) * BLOCK : n * BLOCK] = dot(folding, over).astype(
                    jnp.bfloat16
                )
    wide = TOK - BLOCK
    rows = iota((wide, 1), 0, BLOCK)
    swap = one_hot(iota((wide, TOK), 1) == 2 * starts(bounds, rows) + 256 - rows)
    moved = dot(over_ref[...], swap)
    out_ref[: heads * HD, :] = (out_ref[: heads * HD, :].astype(jnp.float32) + moved).astype(
        jnp.bfloat16
    )
    out_ref[heads * HD :, :] = diagonal_ref[...].astype(jnp.bfloat16)


def unpack_kernel(heads, place_ref, packed_ref, grad_ref, segment_ref, own_ref, given_ref):
    bounds = boundaries(segment_ref[pl.ds(place_ref[1], 1), :])
    core = place_ref[2]
    base = place_ref[3]
    below = iota((BLOCK, BLOCK), 0) < iota((BLOCK, BLOCK), 1)
    level = iota((BLOCK, BLOCK), 0) == iota((BLOCK, BLOCK), 1)
    above = iota((BLOCK, BLOCK), 0) > iota((BLOCK, BLOCK), 1)
    wide = TOK - BLOCK
    queries = iota((1, wide), 1, BLOCK)
    swap = one_hot(iota((TOK, wide), 0) == 2 * starts(bounds, queries) + 256 - queries)
    over = dot(packed_ref[: heads * HD, :], swap).astype(jnp.bfloat16)
    probs = {}
    for n in range(BLOCKS):
        low, count = window(n)
        here = slice(n * BLOCK, (n + 1) * BLOCK)
        visible = seen(bounds, n)
        if n:
            rows = iota(((n - low) * BLOCK, 1), 0, low * BLOCK)
            shifted = iota((1, BLOCK), 1) + rows - 2 * starts(bounds, rows) - 127
            unfolding = one_hot((shifted & 127) == 0)
        for h in range(heads):
            features = slice(h * HD, (h + 1) * HD)
            kept = packed_ref[features, here].astype(jnp.float32)
            level_row = packed_ref[heads * HD : heads * HD + 16, here].astype(jnp.float32)[h : h + 1]
            parts = [jnp.where(below, kept, jnp.where(level, level_row, 0.0))]
            if n:
                found = dot(unfolding, over[features, (n - 1) * BLOCK : n * BLOCK])
                parts = [jnp.where(below, found[-BLOCK:], kept)] + parts
            if n > 1:
                parts = [jnp.where(above, found[:BLOCK], 0.0)] + parts
            for m, part in enumerate(parts):
                shown = jnp.where(visible[m * BLOCK : (m + 1) * BLOCK], part, 0.0)
                probs[h, low + m, n] = shown.astype(jnp.bfloat16)
    half = BLOCK // 2
    for m in range(BLOCKS):
        place = pl.multiple_of(lax.rem(m - base + BLOCKS, BLOCKS) * half, half)
        last = min(m + 3, BLOCKS)
        for h in range(heads):
            features = slice(h * HD, (h + 1) * HD)
            left = jnp.concatenate([probs[h, m, n] for n in range(m, last)], 1)
            grad = dot(left, grad_ref[0, m * BLOCK : last * BLOCK, features])
            own_ref[pl.ds(place, half), features] = jnp.where(
                core == 0, grad[:half], grad[half:]
            ).astype(jnp.bfloat16)
            given_ref[pl.ds(place, half), features] = jnp.where(
                core == 0, grad[half:], grad[:half]
            ).astype(jnp.bfloat16)


def packed_probs(place, stashed, segment_ids, first, heads):
    width = heads * HD
    return pl.pallas_call(
        functools.partial(pack_kernel, heads),
        out_shape=jax.ShapeDtypeStruct((width + 16, TOK), jnp.bfloat16),
        grid_spec=pltpu.PrefetchScalarGridSpec(
            num_scalar_prefetch=1,
            grid=(1,),
            in_specs=[
                pl.BlockSpec((1, 2, TOK, width), lambda i, p: (0, 0, 0, first // heads)),
                pl.BlockSpec((32, TOK), lambda i, p: (0, 0)),
            ],
            out_specs=pl.BlockSpec((width + 16, TOK), lambda i, p: (0, 0)),
            scratch_shapes=[
                pltpu.VMEM((width, TOK - BLOCK), jnp.bfloat16),
                pltpu.VMEM((16, TOK), jnp.float32),
            ],
        ),
        compiler_params=pltpu.CompilerParams(vmem_limit_bytes=VMEM),
    )(place, stashed, segment_ids)


def value_gradient(place, packed, grad_heads, segment_ids, first, heads):
    width = heads * HD
    out = jax.ShapeDtypeStruct((TOK // 2, width), jnp.bfloat16)
    return pl.pallas_call(
        functools.partial(unpack_kernel, heads),
        out_shape=(out, out),
        grid_spec=pltpu.PrefetchScalarGridSpec(
            num_scalar_prefetch=1,
            grid=(1,),
            in_specs=[
                pl.BlockSpec((width + 16, TOK), lambda i, p: (0, 0)),
                pl.BlockSpec((1, TOK, width), lambda i, p: (0, 0, first // heads)),
                pl.BlockSpec((32, TOK), lambda i, p: (0, 0)),
            ],
            out_specs=(
                pl.BlockSpec((TOK // 2, width), lambda i, p: (0, 0)),
                pl.BlockSpec((TOK // 2, width), lambda i, p: (0, 0)),
            ),
        ),
        compiler_params=pltpu.CompilerParams(vmem_limit_bytes=VMEM),
    )(place, packed, grad_heads, segment_ids)


def product_kernel(own_ref, taken_ref, weight_ref, other_ref, up_ref, down_ref, near_ref):
    sums = dot(own_ref[...], weight_ref[0], NT) + dot(taken_ref[...], other_ref[...], NT)
    up_ref[...] = sums[64:128].astype(jnp.bfloat16)
    down_ref[...] = sums[128:192].astype(jnp.bfloat16)
    near_ref[:64] = sums[:64]
    near_ref[64:] = sums[192:]


def products(own, taken, weight, other_weight, start, width):
    sent_shape = jax.ShapeDtypeStruct((64, width), jnp.bfloat16)
    first = start // TILE
    rows, heads = own.shape
    return pl.pallas_call(
        product_kernel,
        out_shape=(sent_shape, sent_shape, jax.ShapeDtypeStruct((128, width), jnp.float32)),
        grid=(width // TILE,),
        in_specs=[
            pl.BlockSpec((rows, heads), lambda i: (0, 0)),
            pl.BlockSpec((rows, heads), lambda i: (0, 0)),
            pl.BlockSpec((1, TILE, heads), lambda i: (0, first + i, 0)),
            pl.BlockSpec((TILE, heads), lambda i: (first + i, 0)),
        ],
        out_specs=(
            pl.BlockSpec((64, TILE), lambda i: (0, i)),
            pl.BlockSpec((64, TILE), lambda i: (0, i)),
            pl.BlockSpec((128, TILE), lambda i: (0, i)),
        ),
        compiler_params=pltpu.CompilerParams(vmem_limit_bytes=VMEM),
    )(own, taken, weight, other_weight)


def body(stashed_qk, grad_heads, segment_ids, w_value, grad_in):
    section = lax.axis_index("section")
    tensor = lax.axis_index("tensor")
    z_low, z_high, core = section % 2, tensor // 2, tensor % 2
    piece = FEAT // PIECES
    base = (z_high + z_low) % BLOCKS
    place = jnp.stack([31 - section, section, core, base]).astype(jnp.int32)

    weight = w_value[0]
    other_weight = sent(weight, other_core)
    packed = [
        sent(packed_probs(place, stashed_qk, segment_ids, *group), mirror) for group in GROUPS
    ]
    own, taken = [], []
    for group, probs in zip(GROUPS, packed):
        kept, given = value_gradient(place, probs, grad_heads, segment_ids, *group)
        own.append(kept)
        taken.append(sent(given, other_core))
    own = jnp.concatenate(own, 1)
    taken = jnp.concatenate(taken, 1)

    far, near = [], []
    for n in range(PIECES):
        up, down, rest = products(own, taken, w_value, other_weight, n * piece, piece)
        far.append((sent(up, along_z(2)), sent(down, along_z(-2))))
        near.append(rest)
    pieces = []
    for n in range(PIECES):
        added = grad_in[0][:, n * piece : (n + 1) * piece].astype(jnp.float32)
        up = near[n][:64] + far[n][0].astype(jnp.float32) + jnp.where(z_low == 0, added, 0.0)
        down = near[n][64:] + far[n][1].astype(jnp.float32) + jnp.where(z_low == 1, added, 0.0)
        risen = sent(up.astype(jnp.bfloat16), to_previous(1))
        fallen = sent(down.astype(jnp.bfloat16), to_previous(-1))
        pieces.append((risen.astype(jnp.float32) + fallen.astype(jnp.float32)).astype(jnp.bfloat16))
    return jnp.concatenate(pieces, 1)[None]


def solution(mesh):
    in_specs = (
        P("section", None, None, "tensor"),
        P("section", None, "tensor"),
        P(),
        P("section", None, "tensor"),
        P("section", "tensor", None),
    )
    out_specs = P("section", "tensor", None)
    return jax.shard_map(body, mesh=mesh, in_specs=in_specs, out_specs=out_specs, check_vma=False)
```

```python
import functools

import jax
import jax.numpy as jnp
from jax import lax
from jax.experimental import pallas as pl
from jax.experimental.pallas import tpu as pltpu
from jax.sharding import PartitionSpec as P

HD = 128
TOK = 512
FEAT = 6144
AXES = ("section", "tensor")
GROUPS = ((0, 2), (2, 2), (4, 2))
PIECES = 4
TILE = 768
BLOCK = 128
BLOCKS = TOK // BLOCK
NT = (((1,), (1,)), ((), ()))
NN = (((1,), (0,)), ((), ()))
VMEM = 48 * 1024 * 1024


def place_of(device):
    section, tensor = divmod(device, 8)
    return section // 8, section // 2 % 4, tensor // 2 * 2 + section % 2, tensor % 2


def device_at(y, x, z, core):
    section = (y % 4) * 8 + (x % 4) * 2 + z % 2
    return section * 8 + z % 8 // 2 * 2 + core


def sent(value, target):
    pairs = []
    for device in range(256):
        place = target(*place_of(device))
        if place is not None:
            pairs.append((device, device_at(*place)))
    return lax.ppermute(value, AXES, pairs)


def mirror(y, x, z, core):
    return 3 - y, 3 - x, z ^ 1, core


def other_core(y, x, z, core):
    return y, x, z, 1 - core


def along_z(by):
    return lambda y, x, z, core: (y, x, z + by, core)


def to_previous(by):
    def target(y, x, z, core):
        if z % 2 == 1:
            return y, x, z + by, core
        if x > 0:
            return y, x - 1, z + by, core
        return (y - 1, 3, z + by, core) if y > 0 else None

    return target


def iota(shape, dim, start=0):
    return lax.broadcasted_iota(jnp.int32, shape, dim) + start


def boundaries(row):
    return [
        jnp.sum(jnp.where(row < n, 1.0, 0.0), axis=1, keepdims=True).astype(jnp.int32)
        for n in (1, 2, 3)
    ]


def starts(bounds, positions):
    found = jnp.zeros_like(positions)
    for bound in bounds:
        found = jnp.where(positions >= bound, bound, found)
    return found


def dot(left, right, dims=NN):
    return lax.dot_general(left, right, dims, preferred_element_type=jnp.float32)


def one_hot(condition):
    return jnp.where(condition, 1.0, 0.0).astype(jnp.bfloat16)


def window(n):
    low = max(n - 2, 0)
    return low, n - low + 1


def seen(bounds, n):
    low, count = window(n)
    keys = iota((count * BLOCK, BLOCK), 0, low * BLOCK)
    rows = iota((1, BLOCK), 1, n * BLOCK)
    return (keys >= starts(bounds, rows)) & (keys <= rows)


def pack_kernel(heads, place_ref, stash_ref, segment_ref, out_ref, over_ref, diagonal_ref):
    bounds = boundaries(segment_ref[pl.ds(place_ref[0], 1), :])
    below = iota((BLOCK, BLOCK), 0) < iota((BLOCK, BLOCK), 1)
    level = iota((BLOCK, BLOCK), 0) == iota((BLOCK, BLOCK), 1)
    above = iota((BLOCK, BLOCK), 0) > iota((BLOCK, BLOCK), 1)
    diagonal_ref[...] = jnp.zeros_like(diagonal_ref)
    factor = HD ** (-0.5) * 1.4426950408889634
    for n in range(BLOCKS):
        low, count = window(n)
        here = slice(n * BLOCK, (n + 1) * BLOCK)
        bias = jnp.where(seen(bounds, n), 0.0, -1e30)
        if n:
            columns = iota((1, n * BLOCK - low * BLOCK), 1, low * BLOCK)
            shifted = iota((BLOCK, 1), 0) + columns - 2 * starts(bounds, columns) - 127
            folding = one_hot((shifted & 127) == 0)
        for h in range(heads):
            features = slice(h * HD, (h + 1) * HD)
            keys = stash_ref[0, 1, low * BLOCK : (n + 1) * BLOCK, features]
            scores = dot(keys, stash_ref[0, 0, here, features], NT) + bias
            largest = jnp.max(scores, axis=0, keepdims=True)
            raised = jnp.exp2((scores - largest) * factor)
            probs = raised * (1.0 / jnp.sum(raised, axis=0, keepdims=True))
            last = probs[(count - 1) * BLOCK :]
            second = probs[(count - 2) * BLOCK : (count - 1) * BLOCK] if n else None
            first = probs[:BLOCK] if n > 1 else None
            diagonal_ref[h : h + 1, here] = jnp.sum(
                jnp.where(level, last, 0.0), axis=0, keepdims=True
            )
            kept = jnp.where(below, last, second if n else 0.0)
            out_ref[features, here] = kept.astype(jnp.bfloat16)
            if n:
                over = jnp.where(below, second, 0.0).astype(jnp.bfloat16)
                if n > 1:
                    over = jnp.concatenate(
                        [jnp.where(above, first, 0.0).astype(jnp.bfloat16), over], 0
                    )
                over_ref[features, (n - 1) * BLOCK : n * BLOCK] = dot(folding, over).astype(
                    jnp.bfloat16
                )
    wide = TOK - BLOCK
    rows = iota((wide, 1), 0, BLOCK)
    swap = one_hot(iota((wide, TOK), 1) == 2 * starts(bounds, rows) + 256 - rows)
    moved = dot(over_ref[...], swap)
    out_ref[: heads * HD, :] = (out_ref[: heads * HD, :].astype(jnp.float32) + moved).astype(
        jnp.bfloat16
    )
    out_ref[heads * HD :, :] = diagonal_ref[...].astype(jnp.bfloat16)


def unpack_kernel(heads, place_ref, packed_ref, grad_ref, segment_ref, own_ref, given_ref):
    bounds = boundaries(segment_ref[pl.ds(place_ref[1], 1), :])
    core = place_ref[2]
    base = place_ref[3]
    below = iota((BLOCK, BLOCK), 0) < iota((BLOCK, BLOCK), 1)
    level = iota((BLOCK, BLOCK), 0) == iota((BLOCK, BLOCK), 1)
    above = iota((BLOCK, BLOCK), 0) > iota((BLOCK, BLOCK), 1)
    wide = TOK - BLOCK
    queries = iota((1, wide), 1, BLOCK)
    swap = one_hot(iota((TOK, wide), 0) == 2 * starts(bounds, queries) + 256 - queries)
    over = dot(packed_ref[: heads * HD, :], swap).astype(jnp.bfloat16)
    probs = {}
    for n in range(BLOCKS):
        low, count = window(n)
        here = slice(n * BLOCK, (n + 1) * BLOCK)
        visible = seen(bounds, n)
        if n:
            rows = iota(((n - low) * BLOCK, 1), 0, low * BLOCK)
            shifted = iota((1, BLOCK), 1) + rows - 2 * starts(bounds, rows) - 127
            unfolding = one_hot((shifted & 127) == 0)
        for h in range(heads):
            features = slice(h * HD, (h + 1) * HD)
            kept = packed_ref[features, here].astype(jnp.float32)
            level_row = packed_ref[heads * HD : heads * HD + 16, here].astype(jnp.float32)[h : h + 1]
            parts = [jnp.where(below, kept, jnp.where(level, level_row, 0.0))]
            if n:
                found = dot(unfolding, over[features, (n - 1) * BLOCK : n * BLOCK])
                parts = [jnp.where(below, found[-BLOCK:], kept)] + parts
            if n > 1:
                parts = [jnp.where(above, found[:BLOCK], 0.0)] + parts
            for m, part in enumerate(parts):
                shown = jnp.where(visible[m * BLOCK : (m + 1) * BLOCK], part, 0.0)
                probs[h, low + m, n] = shown.astype(jnp.bfloat16)
    half = BLOCK // 2
    for m in range(BLOCKS):
        place = pl.multiple_of(lax.rem(m - base + BLOCKS, BLOCKS) * half, half)
        last = min(m + 3, BLOCKS)
        for h in range(heads):
            features = slice(h * HD, (h + 1) * HD)
            left = jnp.concatenate([probs[h, m, n] for n in range(m, last)], 1)
            grad = dot(left, grad_ref[0, m * BLOCK : last * BLOCK, features])
            own_ref[pl.ds(place, half), features] = jnp.where(
                core == 0, grad[:half], grad[half:]
            ).astype(jnp.bfloat16)
            given_ref[pl.ds(place, half), features] = jnp.where(
                core == 0, grad[half:], grad[:half]
            ).astype(jnp.bfloat16)


def packed_probs(place, stashed, segment_ids, first, heads):
    width = heads * HD
    return pl.pallas_call(
        functools.partial(pack_kernel, heads),
        out_shape=jax.ShapeDtypeStruct((width + 16, TOK), jnp.bfloat16),
        grid_spec=pltpu.PrefetchScalarGridSpec(
            num_scalar_prefetch=1,
            grid=(1,),
            in_specs=[
                pl.BlockSpec((1, 2, TOK, width), lambda i, p: (0, 0, 0, first // heads)),
                pl.BlockSpec((32, TOK), lambda i, p: (0, 0)),
            ],
            out_specs=pl.BlockSpec((width + 16, TOK), lambda i, p: (0, 0)),
            scratch_shapes=[
                pltpu.VMEM((width, TOK - BLOCK), jnp.bfloat16),
                pltpu.VMEM((16, TOK), jnp.float32),
            ],
        ),
        compiler_params=pltpu.CompilerParams(vmem_limit_bytes=VMEM),
    )(place, stashed, segment_ids)


def value_gradient(place, packed, grad_heads, segment_ids, first, heads):
    width = heads * HD
    out = jax.ShapeDtypeStruct((TOK // 2, width), jnp.bfloat16)
    return pl.pallas_call(
        functools.partial(unpack_kernel, heads),
        out_shape=(out, out),
        grid_spec=pltpu.PrefetchScalarGridSpec(
            num_scalar_prefetch=1,
            grid=(1,),
            in_specs=[
                pl.BlockSpec((width + 16, TOK), lambda i, p: (0, 0)),
                pl.BlockSpec((1, TOK, width), lambda i, p: (0, 0, first // heads)),
                pl.BlockSpec((32, TOK), lambda i, p: (0, 0)),
            ],
            out_specs=(
                pl.BlockSpec((TOK // 2, width), lambda i, p: (0, 0)),
                pl.BlockSpec((TOK // 2, width), lambda i, p: (0, 0)),
            ),
        ),
        compiler_params=pltpu.CompilerParams(vmem_limit_bytes=VMEM),
    )(place, packed, grad_heads, segment_ids)


def product_kernel(own_ref, taken_ref, weight_ref, other_ref, up_ref, down_ref, near_ref):
    sums = dot(own_ref[...], weight_ref[0], NT) + dot(taken_ref[...], other_ref[...], NT)
    up_ref[...] = sums[64:128].astype(jnp.bfloat16)
    down_ref[...] = sums[128:192].astype(jnp.bfloat16)
    near_ref[:64] = sums[:64]
    near_ref[64:] = sums[192:]


def products(own, taken, weight, other_weight, start, width):
    sent_shape = jax.ShapeDtypeStruct((64, width), jnp.bfloat16)
    first = start // TILE
    rows, heads = own.shape
    return pl.pallas_call(
        product_kernel,
        out_shape=(sent_shape, sent_shape, jax.ShapeDtypeStruct((128, width), jnp.float32)),
        grid=(width // TILE,),
        in_specs=[
            pl.BlockSpec((rows, heads), lambda i: (0, 0)),
            pl.BlockSpec((rows, heads), lambda i: (0, 0)),
            pl.BlockSpec((1, TILE, heads), lambda i: (0, first + i, 0)),
            pl.BlockSpec((TILE, heads), lambda i: (first + i, 0)),
        ],
        out_specs=(
            pl.BlockSpec((64, TILE), lambda i: (0, i)),
            pl.BlockSpec((64, TILE), lambda i: (0, i)),
            pl.BlockSpec((128, TILE), lambda i: (0, i)),
        ),
        compiler_params=pltpu.CompilerParams(vmem_limit_bytes=VMEM),
    )(own, taken, weight, other_weight)


def body(stashed_qk, grad_heads, segment_ids, w_value, grad_in):
    section = lax.axis_index("section")
    tensor = lax.axis_index("tensor")
    z_low, z_high, core = section % 2, tensor // 2, tensor % 2
    piece = FEAT // PIECES
    base = (z_high + z_low) % BLOCKS
    place = jnp.stack([31 - section, section, core, base]).astype(jnp.int32)

    weight = w_value[0]
    other_weight = sent(weight, other_core)
    packed = [
        sent(packed_probs(place, stashed_qk, segment_ids, *group), mirror) for group in GROUPS
    ]
    own, taken = [], []
    for group, probs in zip(GROUPS, packed):
        kept, given = value_gradient(place, probs, grad_heads, segment_ids, *group)
        own.append(kept)
        taken.append(sent(given, other_core))
    own = jnp.concatenate(own, 1)
    taken = jnp.concatenate(taken, 1)

    far, near = [], []
    for n in range(PIECES):
        up, down, rest = products(own, taken, w_value, other_weight, n * piece, piece)
        far.append((sent(up, along_z(2)), sent(down, along_z(-2))))
        near.append(rest)
    pieces = []
    for n in range(PIECES):
        added = grad_in[0][:, n * piece : (n + 1) * piece].astype(jnp.float32)
        up = near[n][:64] + far[n][0].astype(jnp.float32) + jnp.where(z_low == 0, added, 0.0)
        down = near[n][64:] + far[n][1].astype(jnp.float32) + jnp.where(z_low == 1, added, 0.0)
        risen = sent(up.astype(jnp.bfloat16), to_previous(1))
        fallen = sent(down.astype(jnp.bfloat16), to_previous(-1))
        pieces.append((risen.astype(jnp.float32) + fallen.astype(jnp.float32)).astype(jnp.bfloat16))
    return jnp.concatenate(pieces, 1)[None]


def solution(mesh):
    in_specs = (
        P("section", None, None, "tensor"),
        P("section", None, "tensor"),
        P(),
        P("section", None, "tensor"),
        P("section", "tensor", None),
    )
    out_specs = P("section", "tensor", None)
    return jax.shard_map(body, mesh=mesh, in_specs=in_specs, out_specs=out_specs, check_vma=False)
```
